256 devices in a mesh: sym: 8 (over z_hi, core), rad: 32 (over z_lo, x, y).
Axes of the slice: x: 4, y: 4, z: 8 (z_hi: 4, z_lo: 2; z = z_hi * 2 + z_lo), core: 2. Of those that a mesh axis runs over, the one named last changes fastest.
Arguments:
- start_amplitudes: float32 [8, 768, 32, 128], P('sym', None, 'rad'), may hold values from -6 to 6
- coupling: bfloat16 [8, 3, 768, 3, 768], P('sym'), may hold values from -0.078125 to 0.078125
- block_pattern: int32 [8, 6, 3, 6], P('sym'), may hold values 0 or 1
- counts: int32 [8], P('sym'), may hold values from 256 to 768, as said below
- radial_terms: float32 [3, 512], P(None, 'rad'), may hold values from 0.5 to 2
- energy: float32 [8, 768], P('sym'), may hold values from -3 to 3
- potential: float32 [512], replicated, may hold values from -3.140625 to 3.140625
- element_matrices: float32 [2, 4, 128, 128], replicated, may hold values from -0.375 to 0.375
Outputs:
- end_amplitudes: float32 [8, 768, 32, 128], P('sym', None, 'rad')
The draws below stay inside these ranges and needn't reach their ends.
Inputs may be any that keep to these rules, and one draw needn't show every extreme that they name: `counts`: some symmetry has exactly 768 live channels in every draw.
All inputs are finite; a program needn't handle non-finite values. No bound on the sum of `block_pattern` on one device may be relied on, other than what follows from the above.
Results may differ from the reference program's by a relative error of at most 0.0029.
Values may be sent and summed in bfloat16 or wider, within the bound.
A program may use at most 128 MiB of HBM per device.

```python
import math
import jax
import jax.numpy as jnp
from jax import lax

CHANNELS = 768
ORDERS = 3
PATTERN_TILE = 128
ELEM_WIDTH = 128
RAD_DEV = 16
STATES = 4
TIME_STEPS = 2
SYMMETRIES = 8
RAD_BLOCKS = 32
COLUMNS = 128
POINTS = 512
ELEMENTS = 4


def draw_counts(key, part):
    first_key = jax.random.fold_in(key, 11)
    second_key = jax.random.fold_in(key, 23)
    values = jax.random.randint(first_key, (SYMMETRIES,), CHANNELS // 3, CHANNELS + 1)
    chosen = jax.random.randint(second_key, (), 0, SYMMETRIES)
    return jnp.where(jnp.arange(SYMMETRIES) == chosen, CHANNELS, values).astype(jnp.int32)


def set_ends(values, key, least, largest):
    shape = values.shape
    index_at = [jax.random.randint(jax.random.fold_in(key, axis), (), 0, shape[axis]) for axis in range(len(shape))]
    values = values.at[tuple(index_at)].set(least)
    longest = shape.index(max(shape))
    index_at[longest] = (index_at[longest] + 1) % shape[longest]
    return values.at[tuple(index_at)].set(largest)


def block_levels(key, dims, shards, least, top_value):
    level = 1.0
    for dim, shards_of in shards:
        draws = jax.random.uniform(jax.random.fold_in(jax.random.fold_in(key, 6), dim), (shards_of,), jnp.float32, least / len(shards), top_value / len(shards))
        level = level * jnp.repeat(jnp.exp(draws), dims[dim] // shards_of).reshape((-1,) + (1,) * (len(dims) - 1 - dim))
    return level


def centred(stream_key, dims, scale, most, pieces=(), kind=jnp.bfloat16):
    values = jax.random.normal(stream_key, dims, jnp.float32) * scale
    if len(pieces) > 0:
        values = block_levels(stream_key, dims, pieces, -0.22, 0.18) * values
    return jnp.clip(values, min=-most, max=most).astype(kind)


def setup_inputs(seed: int = 0) -> dict:
    key_of = jax.random.split(jax.random.key(seed), 9)
    start_amplitudes = centred(key_of[0], (SYMMETRIES, CHANNELS, RAD_BLOCKS, COLUMNS), 1.0, 6.0, ((0, 8), (2, 32)), jnp.float32)
    coupling = centred(key_of[1], (SYMMETRIES, ORDERS, CHANNELS, 3, CHANNELS), (3 * ORDERS * CHANNELS) ** -0.5, 0.078125, ((0, 8),))
    block_pattern = set_ends((jax.random.randint(key_of[2], (SYMMETRIES, CHANNELS // PATTERN_TILE, 3, CHANNELS // PATTERN_TILE), 0, 4) < 3).astype(jnp.int32), jax.random.fold_in(key_of[2], 1), 0, 1)
    counts = draw_counts(jax.random.fold_in(key_of[8], 71), 0)
    radial_terms = jnp.clip(jnp.exp(math.log(2.0) - 1.3862944 * jax.random.uniform(key_of[4], (ORDERS, POINTS), jnp.float32) ** block_levels(key_of[4], (ORDERS, POINTS), ((1, 32),), -0.2, 0.2)), 0.5, 2.0)
    energy = jnp.clip(jax.random.uniform(key_of[5], (SYMMETRIES, CHANNELS), jnp.float32, -3.0, 3.0) * block_levels(key_of[5], (SYMMETRIES, CHANNELS), ((0, 8),), -0.4, 0.0), -3.0, 3.0)
    potential = jnp.clip(jax.random.uniform(key_of[6], (POINTS,), jnp.float32, -3.140625, 3.140625), -3.140625, 3.140625)
    element_matrices = centred(key_of[7], (2, ELEMENTS, ELEM_WIDTH, ELEM_WIDTH), (2 * ELEM_WIDTH) ** -0.5, 0.375, (), jnp.float32)
    return {"start_amplitudes": start_amplitudes, "coupling": coupling, "block_pattern": block_pattern, "counts": counts, "radial_terms": radial_terms, "energy": energy, "potential": potential, "element_matrices": element_matrices}


step_length = 0.8


def element_product(real_part, imag_part, matrices):
    shape_in = real_part.shape
    elements = matrices.shape[1]
    width = matrices.shape[2]
    real_blocks = real_part.reshape(shape_in[:-1] + (elements, width))
    imag_blocks = imag_part.reshape(shape_in[:-1] + (elements, width))
    highest = lax.Precision.HIGHEST
    out_real = jnp.einsum("abnej,eij->abnei", real_blocks, matrices[0], precision=highest) - jnp.einsum("abnej,eij->abnei", imag_blocks, matrices[1], precision=highest)
    out_imag = jnp.einsum("abnej,eij->abnei", imag_blocks, matrices[0], precision=highest) + jnp.einsum("abnej,eij->abnei", real_blocks, matrices[1], precision=highest)
    return out_real.reshape(shape_in), out_imag.reshape(shape_in)


def radial_half(channel_block, cosine, sine, matrices):
    real_part = channel_block[:, :, :, 0, :]
    imag_part = channel_block[:, :, :, 1, :]
    turned_real = real_part * cosine + imag_part * sine
    turned_imag = imag_part * cosine - real_part * sine
    out_real, out_imag = element_product(turned_real, turned_imag, matrices)
    return jnp.stack((out_real, out_imag), axis=3)


def to_points(stored):
    split = stored.reshape(SYMMETRIES, CHANNELS, RAD_BLOCKS, STATES, 2, RAD_DEV)
    return split.transpose(0, 1, 3, 4, 2, 5).reshape(SYMMETRIES, CHANNELS, STATES, 2, POINTS)


def to_blocks(amplitudes):
    split = amplitudes.reshape(SYMMETRIES, CHANNELS, STATES, 2, RAD_BLOCKS, RAD_DEV)
    return split.transpose(0, 1, 4, 2, 3, 5).reshape(SYMMETRIES, CHANNELS, RAD_BLOCKS, COLUMNS)


def reference(start_amplitudes, coupling, block_pattern, counts, radial_terms, energy, potential, element_matrices):
    live_rows = (jnp.arange(CHANNELS, dtype=jnp.int32)[None, :] < counts[:, None]).astype(jnp.float32)[:, :, None, None, None]
    pattern = jnp.repeat(jnp.repeat(block_pattern, PATTERN_TILE, axis=1), PATTERN_TILE, axis=3).astype(jnp.bfloat16)
    weights = coupling * pattern[:, None]
    angles = energy[:, :, None] + potential[None, None, :]
    cosine = jnp.cos(angles)[:, :, None, :]
    sine = jnp.sin(angles)[:, :, None, :]

    def coupled_term(current):
        padded = jnp.pad(current.astype(jnp.bfloat16), ((1, 1), (0, 0), (0, 0), (0, 0), (0, 0)))

        def one_symmetry(index):
            widened = lax.dynamic_slice_in_dim(padded, index, 3, 0).reshape(3 * CHANNELS, STATES * 2 * POINTS)
            matrix = lax.dynamic_index_in_dim(weights, index, 0, keepdims=False).reshape(ORDERS * CHANNELS, 3 * CHANNELS)
            product = jnp.dot(matrix, widened, preferred_element_type=jnp.float32)
            product = product.reshape(ORDERS, CHANNELS, STATES, 2, POINTS)
            return jnp.sum(product * radial_terms[:, None, None, None, :], axis=0)

        return lax.map(one_symmetry, jnp.arange(SYMMETRIES, dtype=jnp.int32)) * live_rows

    def taylor(amplitudes):
        summed = amplitudes
        current = amplitudes
        for order_index in range(1, 4):
            coupled = coupled_term(current)
            factor = step_length / order_index
            current = jnp.stack((factor * coupled[:, :, :, 1], -factor * coupled[:, :, :, 0]), axis=3)
            summed = summed + current
        return summed

    amplitudes = to_points(start_amplitudes) * live_rows
    for step_index in range(TIME_STEPS):
        amplitudes = radial_half(amplitudes, cosine, sine, element_matrices)
        amplitudes = taylor(amplitudes)
        amplitudes = radial_half(amplitudes, cosine, sine, element_matrices)
    return to_blocks(amplitudes)
```

```python
import jax
import jax.numpy as jnp
from jax import lax
from jax.experimental import pallas as pl
from jax.experimental.pallas import tpu as pltpu
from jax.sharding import PartitionSpec as P

MESH = pl.DeviceIdType.MESH
STEP = 0.8
CH = 768
COLS = 128
HALF = CH // 2
PART = 16
GROUP = 8
ORDERS = 3
TILE = 128
FINE = 256
TERMS = 6
PHASES = 3
SELF, NEAR, FAR = 0, 1, 2
F32 = jnp.float32
BF16 = jnp.bfloat16


def split(x):
    high = x.astype(BF16)
    return high, (x - high.astype(F32)).astype(BF16)


def kernel(
    counts, pattern, start, coupling, radial, energy, potential, matrices,
    out,
    raw, wt, xbuf, rin, rout, vt, vback, acc, even, odd, cosine, sine, start_v, mat_v, bhigh, blow, rad_t,
    load_sem, w_sem, in_send, in_recv, out_send, out_recv, near_send, near_recv, far_send, far_recv,
):
    s = lax.axis_index("sym")
    q = lax.axis_index("rad")
    e = q // GROUP
    g = q % GROUP
    above_near = s % 2 == 0
    near = jnp.where(above_near, s + 1, s - 1)
    far = jnp.where(above_near, s - 1, s + 1)
    has_far = jnp.logical_and(far >= 0, far < 8)
    k_near = jnp.where(above_near, 2, 0)
    k_far = jnp.where(above_near, 0, 2)

    start_load = pltpu.make_async_copy(start, start_v, load_sem.at[0])
    start_load.start()
    mat_load = pltpu.make_async_copy(matrices.at[:, e], mat_v, load_sem.at[1])
    mat_load.start()
    w_loads = [pltpu.make_async_copy(coupling.at[i], raw.at[i], w_sem.at[i]) for i in range(9)]
    for load in w_loads:
        load.start()

    def peer(d):
        return (g + d) % GROUP

    def peer_back(d):
        return (g + GROUP - d) % GROUP

    barrier = pltpu.get_barrier_semaphore()
    for d in range(1, GROUP):
        pl.semaphore_signal(barrier, inc=1, device_id=(s, e * GROUP + peer(d)), device_id_type=MESH)
    pl.semaphore_signal(barrier, inc=1, device_id=(near, q), device_id_type=MESH)

    @pl.when(has_far)
    def _():
        pl.semaphore_signal(barrier, inc=1, device_id=(far, q), device_id_type=MESH)

    def rows_of(i):
        return pl.ds(pl.multiple_of((i // 2) * 2 * PART, 2 * PART), 2 * PART)

    def lanes_of(i):
        return pl.ds(pl.multiple_of((i % 2) * HALF, HALF), HALF)

    def in_copy(phase, d):
        i = peer(d)
        return pltpu.make_async_remote_copy(
            src_ref=vt.at[phase, rows_of(i), lanes_of(i)],
            dst_ref=rin.at[phase, g],
            send_sem=in_send.at[phase, d],
            recv_sem=in_recv.at[phase, d],
            device_id=(s, e * GROUP + i),
            device_id_type=MESH,
        )

    def out_copy(phase, d):
        i = peer(d)
        return pltpu.make_async_remote_copy(
            src_ref=rout.at[phase, i],
            dst_ref=vback.at[phase, rows_of(g), lanes_of(g)],
            send_sem=out_send.at[phase, d],
            recv_sem=out_recv.at[phase, d],
            device_id=(s, e * GROUP + i),
            device_id_type=MESH,
        )

    def near_copy(t):
        return pltpu.make_async_remote_copy(
            src_ref=xbuf.at[t, SELF],
            dst_ref=xbuf.at[t, NEAR],
            send_sem=near_send.at[t],
            recv_sem=near_recv.at[t],
            device_id=(near, q),
            device_id_type=MESH,
        )

    def far_copy(t, j):
        lanes = pl.ds(j * FINE, FINE)
        return pltpu.make_async_remote_copy(
            src_ref=xbuf.at[t, SELF, :, lanes],
            dst_ref=xbuf.at[t, FAR, :, lanes],
            send_sem=far_send.at[t, j],
            recv_sem=far_recv.at[t, j],
            device_id=(far, q),
            device_id_type=MESH,
        )

    def send_in(phase):
        for d in range(1, GROUP):
            in_copy(phase, d).start()
        rin[phase, g] = vt[phase, rows_of(g), lanes_of(g)]

    def send_far(t, j):
        @pl.when(has_far)
        def _():
            far_copy(t, j).start()

    def wait_far(t, j):
        @pl.when(has_far)
        def _():
            far_copy(t, j).wait_recv()

    start_load.wait()
    lane = lax.broadcasted_iota(jnp.int32, (COLS, CH), 1)
    live = jnp.where(lane < counts[0], 1.0, 0.0).astype(F32)
    for j in range(CH // TILE):
        cols = slice(j * TILE, (j + 1) * TILE)
        vt[0, :, cols] = start_v[cols, :].T * live[:, cols]
    pl.semaphore_wait(barrier, jnp.where(has_far, GROUP + 1, GROUP))
    send_in(0)

    mat_load.wait()
    m0, m1 = mat_v[0], mat_v[1]
    for r, (x, y) in enumerate(((m0, -m1), (m1, m0))):
        for c, part in enumerate((x, y)):
            high, low = split(part)
            bhigh[r * 128 : (r + 1) * 128, c * 128 : (c + 1) * 128] = high
            blow[r * 128 : (r + 1) * 128, c * 128 : (c + 1) * 128] = low
    pot = jnp.broadcast_to(potential[pl.ds(e, 1), :], (TILE, TILE)).T
    for j in range(HALF // TILE):
        lanes = pl.ds(pl.multiple_of((g % 2) * HALF + j * TILE, TILE), TILE)
        angle = energy[:, lanes] + pot
        cosine[:, j * TILE : (j + 1) * TILE] = jnp.cos(angle)
        sine[:, j * TILE : (j + 1) * TILE] = jnp.sin(angle)
    for l in range(ORDERS):
        rad_t[l] = jnp.broadcast_to(radial[l : l + 1, :], (TILE, TILE)).T

    @pl.when(jnp.logical_not(has_far))
    def _():
        for t in range(TERMS):
            xbuf[t, FAR] = jnp.zeros((COLS, CH), BF16)

    def turn_weights(first, last):
        def body(i, _):
            l = i // 3
            k = i % 3
            pltpu.make_async_copy(coupling.at[i], raw.at[i], w_sem.at[i]).wait()
            for a in range(CH // TILE):
                for b in range(CH // TILE):
                    keep = jnp.full((TILE, TILE), pattern[a, k, b].astype(F32), F32).astype(BF16)
                    tile = raw[i, a * TILE : (a + 1) * TILE, b * TILE : (b + 1) * TILE]
                    wt[
                        k,
                        b * TILE : (b + 1) * TILE,
                        pl.ds(pl.multiple_of(l * CH + a * TILE, TILE), TILE),
                    ] = tile.T * keep
            return 0

        lax.fori_loop(first, last, body, 0)

    def element(re, im):
        xhigh, xlow = split(jnp.concatenate((re, im), axis=0))
        y = jnp.dot(bhigh[...], xhigh, preferred_element_type=F32)
        y = y + jnp.dot(bhigh[...], xlow, preferred_element_type=F32)
        y = y + jnp.dot(blow[...], xhigh, preferred_element_type=F32)
        return y[:128], y[128:]

    def turn(re, im):
        c, n = cosine[...], sine[...]
        return re * c + im * n, im * c - re * n

    def radial_phase(phase):
        for d in range(1, GROUP):
            in_copy(phase, d).wait_recv()
        block = rin[phase].reshape(GROUP, 2, PART, HALF)
        re = block[:, 0].reshape(GROUP * PART, HALF)
        im = block[:, 1].reshape(GROUP * PART, HALF)
        re, im = element(*turn(re, im))
        if phase == 1:
            re, im = element(*turn(re, im))
        rout[phase, :, :PART, :] = re.reshape(GROUP, PART, HALF)
        rout[phase, :, PART:, :] = im.reshape(GROUP, PART, HALF)
        for d in range(1, GROUP):
            out_copy(phase, d).start()
        vback[phase, rows_of(g), lanes_of(g)] = rout[phase, g]

    def wait_back(phase):
        for d in range(1, GROUP):
            out_copy(phase, d).wait_recv()

    def term(t, scale, emit):
        acc[...] = jnp.dot(xbuf[t, SELF], wt[1], preferred_element_type=F32)
        near_copy(t).wait_recv()
        acc[...] += jnp.dot(xbuf[t, NEAR], wt[k_near], preferred_element_type=F32)
        wait_far(t, 0)
        wait_far(t, 1)
        acc[...] += jnp.dot(
            xbuf[t, FAR, :, : 2 * FINE], wt[k_far, : 2 * FINE], preferred_element_type=F32
        )
        wait_far(t, 2)
        for j in range(CH // FINE):
            total = None
            for l in range(ORDERS):
                lanes = slice(l * CH + j * FINE, l * CH + (j + 1) * FINE)
                y = acc[:, lanes] + jnp.dot(
                    xbuf[t, FAR, :, 2 * FINE :],
                    wt[k_far, 2 * FINE :, lanes],
                    preferred_element_type=F32,
                )
                factor = jnp.concatenate((rad_t[l], rad_t[l]), axis=1)
                total = y * factor if total is None else total + y * factor
            lane = lax.broadcasted_iota(jnp.int32, (COLS, FINE), 1) + j * FINE
            emit(j, jnp.where(lane < counts[0], total * scale, 0.0))

    def coupling_step(step):
        phase = step
        base = 3 * step
        xbuf[base, SELF] = vback[phase].astype(BF16)
        for j in range(3):
            send_far(base, j)
        near_copy(base).start()

        def first(j, u):
            lanes = slice(j * FINE, (j + 1) * FINE)
            odd[:, lanes] = u
            xbuf[base + 1, SELF, :, lanes] = u.astype(BF16)
            send_far(base + 1, j)

        def second(j, u):
            lanes = slice(j * FINE, (j + 1) * FINE)
            even[:, lanes] = vback[phase, :, lanes] - u
            xbuf[base + 2, SELF, :, lanes] = u.astype(BF16)
            send_far(base + 2, j)

        def third(j, u):
            lanes = slice(j * FINE, (j + 1) * FINE)
            o = odd[:, lanes] - u
            ev = even[:, lanes]
            for n in range(COLS // (2 * PART)):
                a, b, c = n * 2 * PART, n * 2 * PART + PART, (n + 1) * 2 * PART
                vt[phase + 1, a:b, lanes] = ev[a:b] + o[b:c]
                vt[phase + 1, b:c, lanes] = ev[b:c] - o[a:b]

        term(base, STEP, first)
        near_copy(base + 1).start()
        term(base + 1, STEP / 2.0, second)
        near_copy(base + 2).start()
        term(base + 2, STEP / 3.0, third)

    turn_weights(0, 5)
    radial_phase(0)
    turn_weights(5, 9)
    wait_back(0)
    coupling_step(0)
    send_in(1)
    radial_phase(1)
    wait_back(1)
    coupling_step(1)
    send_in(2)
    radial_phase(2)
    wait_back(2)
    for j in range(CH // TILE):
        cols = slice(j * TILE, (j + 1) * TILE)
        out[cols, :] = vback[2, :, cols].T

    for phase in range(PHASES):
        for d in range(1, GROUP):
            in_copy(phase, d).wait_send()
            out_copy(phase, d).wait_send()
    for t in range(TERMS):
        near_copy(t).wait_send()

        @pl.when(has_far)
        def _():
            for j in range(3):
                far_copy(t, j).wait_send()


def shards(
    start_amplitudes, coupling, block_pattern, counts, radial_terms, energy, potential, element_matrices
):
    start = start_amplitudes.reshape(CH, COLS)
    weights = coupling[0].transpose(0, 2, 1, 3).reshape(9, CH, CH)
    radial = jnp.tile(radial_terms, (1, COLS // PART))
    vmem = pl.BlockSpec(memory_space=pltpu.VMEM)
    smem = pl.BlockSpec(memory_space=pltpu.SMEM)
    anywhere = pl.BlockSpec(memory_space=pl.ANY)
    dma = pltpu.SemaphoreType.DMA
    out = pl.pallas_call(
        kernel,
        out_shape=jax.ShapeDtypeStruct((CH, COLS), F32),
        in_specs=[smem, smem, anywhere, anywhere, vmem, vmem, vmem, anywhere],
        out_specs=vmem,
        scratch_shapes=[
            pltpu.VMEM((9, CH, CH), BF16),
            pltpu.VMEM((3, CH, ORDERS * CH), BF16),
            pltpu.VMEM((TERMS, 3, COLS, CH), BF16),
            pltpu.VMEM((PHASES, GROUP, 2 * PART, HALF), F32),
            pltpu.VMEM((PHASES, GROUP, 2 * PART, HALF), F32),
            pltpu.VMEM((PHASES, COLS, CH), F32),
            pltpu.VMEM((PHASES, COLS, CH), F32),
            pltpu.VMEM((COLS, ORDERS * CH), F32),
            pltpu.VMEM((COLS, CH), F32),
            pltpu.VMEM((COLS, CH), F32),
            pltpu.VMEM((TILE, HALF), F32),
            pltpu.VMEM((TILE, HALF), F32),
            pltpu.VMEM((CH, COLS), F32),
            pltpu.VMEM((2, TILE, TILE), F32),
            pltpu.VMEM((2 * TILE, 2 * TILE), BF16),
            pltpu.VMEM((2 * TILE, 2 * TILE), BF16),
            pltpu.VMEM((ORDERS, TILE, TILE), F32),
            dma((2,)),
            dma((9,)),
            dma((PHASES, GROUP)),
            dma((PHASES, GROUP)),
            dma((PHASES, GROUP)),
            dma((PHASES, GROUP)),
            dma((TERMS,)),
            dma((TERMS,)),
            dma((TERMS, 3)),
            dma((TERMS, 3)),
        ],
        compiler_params=pltpu.CompilerParams(
            collective_id=0, has_side_effects=True, vmem_limit_bytes=52 * 2**20
        ),
    )(
        counts,
        block_pattern[0],
        start,
        weights,
        radial,
        energy,
        potential.reshape(4, TILE),
        element_matrices,
    )
    return out.reshape(1, CH, 1, COLS)


def solution(mesh):
    return jax.shard_map(
        shards,
        mesh=mesh,
        in_specs=(
            P("sym", None, "rad", None),
            P("sym", None, None, None, None),
            P("sym", None, None, None),
            P("sym"),
            P(None, "rad"),
            P("sym", None),
            P(),
            P(),
        ),
        out_specs=P("sym", None, "rad", None),
        check_vma=False,
    )
```

```python
import math

import jax
import jax.numpy as jnp
from jax import lax
from jax.experimental import pallas as pl
from jax.experimental.pallas import tpu as pltpu
from jax.sharding import PartitionSpec as P

MESH = pl.DeviceIdType.MESH
STEP = 0.8
CH = 768
COLS = 128
HALF = CH // 2
PART = 16
GROUP = 8
ORDERS = 3
TILE = 128
FINE = 256
TERMS = 6
PHASES = 3
SELF, NEAR, FAR = 0, 1, 2
BLOCK = 7
LEVELS = 64.0
FULL = 32760.0
F32 = jnp.float32
BF16 = jnp.bfloat16


def split(x):
    high = x.astype(BF16)
    return high, (x - high.astype(F32)).astype(BF16)


def pack(re, im, ref):
    rows = lax.broadcasted_iota(jnp.int32, (PART, TILE), 0)
    scales = jnp.zeros((PART, TILE), F32)
    for c in range(HALF // TILE):
        lanes = slice(c * TILE, (c + 1) * TILE)
        a, b = re[:, lanes], im[:, lanes]
        top = jnp.max(jnp.maximum(jnp.abs(a), jnp.abs(b)), axis=0, keepdims=True)
        level = jnp.ceil(jnp.log(jnp.maximum(top, 1e-36)) * (LEVELS / math.log(2.0)))
        factor = jnp.exp2(level * (-1.0 / LEVELS))
        ref[c] = jnp.round(a * factor * FULL).astype(jnp.int32).astype(jnp.int16)
        ref[3 + c] = jnp.round(b * factor * FULL).astype(jnp.int32).astype(jnp.int16)
        scales = jnp.where(rows == c, level, scales)
    ref[6] = scales.astype(jnp.int32).astype(jnp.int16)


def unpack(ref):
    level = ref[6].astype(jnp.int32).astype(F32)
    factor = jnp.exp2(level * (1.0 / LEVELS)) * (1.0 / FULL)
    parts = []
    for first in (0, 3):
        tiles = [
            ref[first + c].astype(jnp.int32).astype(F32) * factor[c : c + 1] for c in range(HALF // TILE)
        ]
        parts.append(jnp.concatenate(tiles, axis=1))
    return parts


def kernel(
    counts, pattern_h, start, coupling, radial_h, energy_h, potential_h, matrices,
    out,
    raw, wt, xbuf, qin, rin, qout, rback, v, acc, even, odd, cosine, sine, start_v, mat_v, bhigh, blow, rad_t,
    pattern, radial, energy, potential, load_sem, w_sem, in_send, in_recv, out_send, out_recv, near_send, near_recv, far_send, far_recv,
):
    s = lax.axis_index("sym")
    q = lax.axis_index("rad")
    e = q // GROUP
    g = q % GROUP
    above_near = s % 2 == 0
    near = jnp.where(above_near, s + 1, s - 1)
    far = jnp.where(above_near, s - 1, s + 1)
    has_far = jnp.logical_and(far >= 0, far < 8)
    k_near = jnp.where(above_near, 2, 0)
    k_far = jnp.where(above_near, 0, 2)

    start_load = pltpu.make_async_copy(start, start_v, load_sem.at[0])
    start_load.start()
    mat_load = pltpu.make_async_copy(matrices.at[:, e], mat_v, load_sem.at[1])
    mat_load.start()
    small_loads = [
        pltpu.make_async_copy(a, b, load_sem.at[2 + i])
        for i, (a, b) in enumerate(
            ((energy_h, energy), (potential_h, potential), (radial_h, radial), (pattern_h, pattern))
        )
    ]
    for load in small_loads:
        load.start()
    w_loads = [pltpu.make_async_copy(coupling.at[i], raw.at[i], w_sem.at[i]) for i in range(9)]
    for load in w_loads:
        load.start()

    def peer(d):
        return (g + d) % GROUP

    def peer_back(d):
        return (g + GROUP - d) % GROUP

    barrier = pltpu.get_barrier_semaphore()
    for d in range(1, GROUP):
        pl.semaphore_signal(barrier, inc=1, device_id=(s, e * GROUP + peer(d)), device_id_type=MESH)
    pl.semaphore_signal(barrier, inc=1, device_id=(near, q), device_id_type=MESH)

    @pl.when(has_far)
    def _():
        pl.semaphore_signal(barrier, inc=1, device_id=(far, q), device_id_type=MESH)

    def in_copy(phase, d):
        i = peer(d)
        return pltpu.make_async_remote_copy(
            src_ref=qin.at[phase, i],
            dst_ref=rin.at[phase, g],
            send_sem=in_send.at[phase, d],
            recv_sem=in_recv.at[phase, d],
            device_id=(s, e * GROUP + i),
            device_id_type=MESH,
        )

    def out_copy(phase, d):
        i = peer(d)
        return pltpu.make_async_remote_copy(
            src_ref=qout.at[phase, i],
            dst_ref=rback.at[phase, g],
            send_sem=out_send.at[phase, d],
            recv_sem=out_recv.at[phase, d],
            device_id=(s, e * GROUP + i),
            device_id_type=MESH,
        )

    def near_copy(t):
        return pltpu.make_async_remote_copy(
            src_ref=xbuf.at[t, SELF],
            dst_ref=xbuf.at[t, NEAR],
            send_sem=near_send.at[t],
            recv_sem=near_recv.at[t],
            device_id=(near, q),
            device_id_type=MESH,
        )

    def far_copy(t, j):
        lanes = pl.ds(j * FINE, FINE)
        return pltpu.make_async_remote_copy(
            src_ref=xbuf.at[t, SELF, :, lanes],
            dst_ref=xbuf.at[t, FAR, :, lanes],
            send_sem=far_send.at[t, j],
            recv_sem=far_recv.at[t, j],
            device_id=(far, q),
            device_id_type=MESH,
        )

    def send_in(phase):
        for i in range(GROUP):
            n, lanes = i // 2, slice((i % 2) * HALF, (i % 2 + 1) * HALF)
            a, b, c = n * 2 * PART, n * 2 * PART + PART, (n + 1) * 2 * PART
            pack(v[a:b, lanes], v[b:c, lanes], qin.at[phase, i])
        for d in range(1, GROUP):
            in_copy(phase, d).start()
        rin[phase, g] = qin[phase, g]

    def send_far(t, j):
        @pl.when(has_far)
        def _():
            far_copy(t, j).start()

    def wait_far(t, j):
        @pl.when(has_far)
        def _():
            far_copy(t, j).wait_recv()

    start_load.wait()
    lane = lax.broadcasted_iota(jnp.int32, (COLS, CH), 1)
    live = jnp.where(lane < counts[0], 1.0, 0.0).astype(F32)
    for j in range(CH // TILE):
        cols = slice(j * TILE, (j + 1) * TILE)
        v[:, cols] = start_v[cols, :].T * live[:, cols]
    pl.semaphore_wait(barrier, jnp.where(has_far, GROUP + 1, GROUP))
    send_in(0)

    for load in small_loads:
        load.wait()
    mat_load.wait()
    m0, m1 = mat_v[0], mat_v[1]
    for r, (x, y) in enumerate(((m0, -m1), (m1, m0))):
        for c, part in enumerate((x, y)):
            high, low = split(part)
            bhigh[r * 128 : (r + 1) * 128, c * 128 : (c + 1) * 128] = high
            blow[r * 128 : (r + 1) * 128, c * 128 : (c + 1) * 128] = low
    pot = jnp.broadcast_to(potential[pl.ds(e, 1), :], (TILE, TILE)).T
    for j in range(HALF // TILE):
        lanes = pl.ds(pl.multiple_of((g % 2) * HALF + j * TILE, TILE), TILE)
        angle = energy[:, lanes] + pot
        cosine[:, j * TILE : (j + 1) * TILE] = jnp.cos(angle)
        sine[:, j * TILE : (j + 1) * TILE] = jnp.sin(angle)
    for l in range(ORDERS):
        rad_t[l] = jnp.concatenate([jnp.broadcast_to(radial[l : l + 1, :], (TILE, PART)).T] * (COLS // PART), axis=0)

    @pl.when(jnp.logical_not(has_far))
    def _():
        for t in range(TERMS):
            xbuf[t, FAR] = jnp.zeros((COLS, CH), BF16)

    def turn_weights(first, last):
        def body(i, _):
            l = i // 3
            k = i % 3
            pltpu.make_async_copy(coupling.at[i], raw.at[i], w_sem.at[i]).wait()
            for a in range(CH // TILE):
                for b in range(CH // TILE):
                    keep = jnp.full((TILE, TILE), pattern[a, k, 0, b].astype(F32), F32).astype(BF16)
                    tile = raw[i, a * TILE : (a + 1) * TILE, b * TILE : (b + 1) * TILE]
                    wt[
                        k,
                        b * TILE : (b + 1) * TILE,
                        pl.ds(pl.multiple_of(l * CH + a * TILE, TILE), TILE),
                    ] = tile.T * keep
            return 0

        lax.fori_loop(first, last, body, 0)

    def element(re, im):
        xhigh, xlow = split(jnp.concatenate((re, im), axis=0))
        y = jnp.dot(bhigh[...], xhigh, preferred_element_type=F32)
        y = y + jnp.dot(bhigh[...], xlow, preferred_element_type=F32)
        y = y + jnp.dot(blow[...], xhigh, preferred_element_type=F32)
        return y[:128], y[128:]

    def turn(re, im):
        c, n = cosine[...], sine[...]
        return re * c + im * n, im * c - re * n

    def radial_phase(phase):
        for d in range(1, GROUP):
            in_copy(phase, d).wait_recv()
        blocks = [unpack(rin.at[phase, i]) for i in range(GROUP)]
        re = jnp.concatenate([b[0] for b in blocks], axis=0)
        im = jnp.concatenate([b[1] for b in blocks], axis=0)
        re, im = element(*turn(re, im))
        if phase == 1:
            re, im = element(*turn(re, im))
        for i in range(GROUP):
            rows = slice(i * PART, (i + 1) * PART)
            pack(re[rows], im[rows], qout.at[phase, i])
        for d in range(1, GROUP):
            out_copy(phase, d).start()
        rback[phase, g] = qout[phase, g]

    def wait_back(phase):
        for d in range(1, GROUP):
            out_copy(phase, d).wait_recv()
        for i in range(GROUP):
            n, lanes = i // 2, slice((i % 2) * HALF, (i % 2 + 1) * HALF)
            a, b, c = n * 2 * PART, n * 2 * PART + PART, (n + 1) * 2 * PART
            v[a:b, lanes], v[b:c, lanes] = unpack(rback.at[phase, i])

    def term(t, scale, emit):
        acc[...] = jnp.dot(xbuf[t, SELF], wt[1], preferred_element_type=F32)
        near_copy(t).wait_recv()
        acc[...] += jnp.dot(xbuf[t, NEAR], wt[k_near], preferred_element_type=F32)
        wait_far(t, 0)
        wait_far(t, 1)
        acc[...] += jnp.dot(
            xbuf[t, FAR, :, : 2 * FINE], wt[k_far, : 2 * FINE], preferred_element_type=F32
        )
        wait_far(t, 2)
        for j in range(CH // FINE):
            total = None
            for l in range(ORDERS):
                lanes = slice(l * CH + j * FINE, l * CH + (j + 1) * FINE)
                y = acc[:, lanes] + jnp.dot(
                    xbuf[t, FAR, :, 2 * FINE :],
                    wt[k_far, 2 * FINE :, lanes],
                    preferred_element_type=F32,
                )
                factor = jnp.concatenate((rad_t[l], rad_t[l]), axis=1)
                total = y * factor if total is None else total + y * factor
            lane = lax.broadcasted_iota(jnp.int32, (COLS, FINE), 1) + j * FINE
            emit(j, jnp.where(lane < counts[0], total * scale, 0.0))

    def coupling_step(step):
        base = 3 * step
        xbuf[base, SELF] = v[...].astype(BF16)
        for j in range(3):
            send_far(base, j)
        near_copy(base).start()

        def first(j, u):
            lanes = slice(j * FINE, (j + 1) * FINE)
            odd[:, lanes] = u
            xbuf[base + 1, SELF, :, lanes] = u.astype(BF16)
            send_far(base + 1, j)

        def second(j, u):
            lanes = slice(j * FINE, (j + 1) * FINE)
            even[:, lanes] = v[:, lanes] - u
            xbuf[base + 2, SELF, :, lanes] = u.astype(BF16)
            send_far(base + 2, j)

        def third(j, u):
            lanes = slice(j * FINE, (j + 1) * FINE)
            o = odd[:, lanes] - u
            ev = even[:, lanes]
            for n in range(COLS // (2 * PART)):
                a, b, c = n * 2 * PART, n * 2 * PART + PART, (n + 1) * 2 * PART
                v[a:b, lanes] = ev[a:b] + o[b:c]
                v[b:c, lanes] = ev[b:c] - o[a:b]

        term(base, STEP, first)
        near_copy(base + 1).start()
        term(base + 1, STEP / 2.0, second)
        near_copy(base + 2).start()
        term(base + 2, STEP / 3.0, third)

    turn_weights(0, 5)
    radial_phase(0)
    turn_weights(5, 9)
    wait_back(0)
    coupling_step(0)
    send_in(1)
    radial_phase(1)
    wait_back(1)
    coupling_step(1)
    send_in(2)
    radial_phase(2)
    wait_back(2)
    for j in range(CH // TILE):
        cols = slice(j * TILE, (j + 1) * TILE)
        out[cols, :] = v[:, cols].T

    for phase in range(PHASES):
        for d in range(1, GROUP):
            in_copy(phase, d).wait_send()
            out_copy(phase, d).wait_send()
    for t in range(TERMS):
        near_copy(t).wait_send()

        @pl.when(has_far)
        def _():
            for j in range(3):
                far_copy(t, j).wait_send()


def shards(
    start_amplitudes, coupling, block_pattern, counts, radial_terms, energy, potential, element_matrices
):
    start = start_amplitudes.reshape(CH, COLS)
    weights = coupling[0].transpose(0, 2, 1, 3).reshape(9, CH, CH)
    vmem = pl.BlockSpec(memory_space=pltpu.VMEM)
    smem = pl.BlockSpec(memory_space=pltpu.SMEM)
    anywhere = pl.BlockSpec(memory_space=pltpu.HBM)
    dma = pltpu.SemaphoreType.DMA
    out = pl.pallas_call(
        kernel,
        out_shape=jax.ShapeDtypeStruct((CH, COLS), F32),
        in_specs=[smem] + [anywhere] * 7,
        out_specs=vmem,
        scratch_shapes=[
            pltpu.VMEM((9, CH, CH), BF16),
            pltpu.VMEM((3, CH, ORDERS * CH), BF16),
            pltpu.VMEM((TERMS, 3, COLS, CH), BF16),
            pltpu.VMEM((PHASES, GROUP, BLOCK, PART, TILE), jnp.int16),
            pltpu.VMEM((PHASES, GROUP, BLOCK, PART, TILE), jnp.int16),
            pltpu.VMEM((PHASES, GROUP, BLOCK, PART, TILE), jnp.int16),
            pltpu.VMEM((PHASES, GROUP, BLOCK, PART, TILE), jnp.int16),
            pltpu.VMEM((COLS, CH), F32),
            pltpu.VMEM((COLS, ORDERS * CH), F32),
            pltpu.VMEM((COLS, CH), F32),
            pltpu.VMEM((COLS, CH), F32),
            pltpu.VMEM((TILE, HALF), F32),
            pltpu.VMEM((TILE, HALF), F32),
            pltpu.VMEM((CH, COLS), F32),
            pltpu.VMEM((2, TILE, TILE), F32),
            pltpu.VMEM((2 * TILE, 2 * TILE), BF16),
            pltpu.VMEM((2 * TILE, 2 * TILE), BF16),
            pltpu.VMEM((ORDERS, TILE, TILE), F32),
            pltpu.SMEM((6, 3, 1, 6), jnp.int32),
            pltpu.VMEM((3, PART), F32),
            pltpu.VMEM((1, CH), F32),
            pltpu.VMEM((4, TILE), F32),
            dma((6,)),
            dma((9,)),
            dma((PHASES, GROUP)),
            dma((PHASES, GROUP)),
            dma((PHASES, GROUP)),
            dma((PHASES, GROUP)),
            dma((TERMS,)),
            dma((TERMS,)),
            dma((TERMS, 3)),
            dma((TERMS, 3)),
        ],
        compiler_params=pltpu.CompilerParams(
            collective_id=0, has_side_effects=True, vmem_limit_bytes=48 * 2**20
        ),
    )(
        counts,
        block_pattern.transpose(1, 2, 0, 3),
        start,
        weights,
        radial_terms,
        energy,
        potential.reshape(4, TILE),
        element_matrices,
    )
    return out.reshape(1, CH, 1, COLS)


def solution(mesh):
    return jax.shard_map(
        shards,
        mesh=mesh,
        in_specs=(
            P("sym", None, "rad", None),
            P("sym", None, None, None, None),
            P("sym", None, None, None),
            P("sym"),
            P(None, "rad"),
            P("sym", None),
            P(),
            P(),
        ),
        out_specs=P("sym", None, "rad", None),
        check_vma=False,
    )
```

```python
import math

import jax
import jax.numpy as jnp
from jax import lax
from jax.experimental import pallas as pl
from jax.experimental.pallas import tpu as pltpu
from jax.sharding import PartitionSpec as P

MESH = pl.DeviceIdType.MESH
STEP = 0.8
CH = 768
COLS = 128
HALF = CH // 2
PART = 16
GROUP = 8
ORDERS = 3
TILE = 128
FINE = 256
TERMS = 6
PHASES = 3
SELF, NEAR, FAR = 0, 1, 2
BLOCK = 7
LEVELS = 64.0
FULL = 32760.0
PARTS = ((0, 2), (2, 4))
F32 = jnp.float32
BF16 = jnp.bfloat16


def rows_in(part):
    first, last = PARTS[part]
    return pl.ds(first * 2 * PART, (last - first) * 2 * PART)


def devices_in(part):
    first, last = PARTS[part]
    return range(2 * first, 2 * last)


def split(x):
    high = x.astype(BF16)
    return high, (x - high.astype(F32)).astype(BF16)


def pack(re, im, ref):
    rows = lax.broadcasted_iota(jnp.int32, (PART, TILE), 0)
    scales = jnp.zeros((PART, TILE), F32)
    for c in range(HALF // TILE):
        lanes = slice(c * TILE, (c + 1) * TILE)
        a, b = re[:, lanes], im[:, lanes]
        top = jnp.max(jnp.maximum(jnp.abs(a), jnp.abs(b)), axis=0, keepdims=True)
        level = jnp.ceil(jnp.log(jnp.maximum(top, 1e-36)) * (LEVELS / math.log(2.0)))
        factor = jnp.exp2(level * (-1.0 / LEVELS))
        ref[c] = jnp.round(a * factor * FULL).astype(jnp.int32).astype(jnp.int16)
        ref[3 + c] = jnp.round(b * factor * FULL).astype(jnp.int32).astype(jnp.int16)
        scales = jnp.where(rows == c, level, scales)
    ref[6] = scales.astype(jnp.int32).astype(jnp.int16)


def unpack(ref):
    level = ref[6].astype(jnp.int32).astype(F32)
    factor = jnp.exp2(level * (1.0 / LEVELS)) * (1.0 / FULL)
    parts = []
    for first in (0, 3):
        tiles = [
            ref[first + c].astype(jnp.int32).astype(F32) * factor[c : c + 1] for c in range(HALF // TILE)
        ]
        parts.append(jnp.concatenate(tiles, axis=1))
    return parts


def kernel(
    counts, pattern_h, start, coupling, radial_h, energy_h, potential_h, matrices,
    out,
    raw, wt, xbuf, hout, qin, rin, qout, rback, v, acc, even, odd, cosine, sine, start_v, mat_v, bhigh, blow, rad_t,
    pattern, radial, energy, potential, load_sem, w_sem, in_send, in_recv, out_send, out_recv, near_send, near_recv,
    far_send, far_recv, direct_send, direct_recv,
):
    s = lax.axis_index("sym")
    q = lax.axis_index("rad")
    e = q // GROUP
    g = q % GROUP
    above_near = s % 2 == 0
    near = jnp.where(above_near, s + 1, s - 1)
    far = jnp.where(above_near, s - 1, s + 1)
    has_far = jnp.logical_and(far >= 0, far < 8)
    k_near = jnp.where(above_near, 2, 0)
    k_far = jnp.where(above_near, 0, 2)

    start_load = pltpu.make_async_copy(start, start_v, load_sem.at[0])
    start_load.start()
    mat_load = pltpu.make_async_copy(matrices.at[:, e], mat_v, load_sem.at[1])
    mat_load.start()
    small_loads = [
        pltpu.make_async_copy(a, b, load_sem.at[2 + i])
        for i, (a, b) in enumerate(
            ((energy_h, energy), (potential_h, potential), (radial_h, radial), (pattern_h, pattern))
        )
    ]
    for load in small_loads:
        load.start()
    w_loads = [pltpu.make_async_copy(coupling.at[i], raw.at[i], w_sem.at[i]) for i in range(9)]
    for load in w_loads:
        load.start()

    barrier = pltpu.get_barrier_semaphore()
    for d in range(1, GROUP):
        pl.semaphore_signal(
            barrier, inc=1, device_id=(s, e * GROUP + (g + d) % GROUP), device_id_type=MESH
        )
    pl.semaphore_signal(barrier, inc=1, device_id=(near, q), device_id_type=MESH)

    @pl.when(has_far)
    def _():
        pl.semaphore_signal(barrier, inc=1, device_id=(far, q), device_id_type=MESH)

    def in_copy(phase, i):
        return pltpu.make_async_remote_copy(
            src_ref=qin.at[phase, i],
            dst_ref=rin.at[phase, g],
            send_sem=in_send.at[phase, i],
            recv_sem=in_recv.at[phase, g],
            device_id=(s, e * GROUP + i),
            device_id_type=MESH,
        )

    def out_copy(phase, i):
        return pltpu.make_async_remote_copy(
            src_ref=qout.at[phase, i],
            dst_ref=rback.at[phase, g],
            send_sem=out_send.at[phase, i],
            recv_sem=out_recv.at[phase, g],
            device_id=(s, e * GROUP + i),
            device_id_type=MESH,
        )

    def wait_block(recv_sem, ref, i):
        @pl.when(g != i)
        def _():
            pltpu.make_async_copy(ref, ref, recv_sem).wait()

    def rows_of(i):
        return pl.ds(pl.multiple_of((i // 2) * 2 * PART, 2 * PART), 2 * PART)

    def lanes_of(i):
        return pl.ds(pl.multiple_of((i % 2) * HALF, HALF), HALF)

    def direct_copy(step, i):
        return pltpu.make_async_remote_copy(
            src_ref=hout.at[step, i],
            dst_ref=xbuf.at[3 * step, FAR, rows_of(g), lanes_of(g)],
            send_sem=direct_send.at[step, i],
            recv_sem=direct_recv.at[step, g],
            device_id=(far, e * GROUP + i),
            device_id_type=MESH,
        )

    def near_copy(t, part):
        rows = rows_in(part)
        return pltpu.make_async_remote_copy(
            src_ref=xbuf.at[t, SELF, rows],
            dst_ref=xbuf.at[t, NEAR, rows],
            send_sem=near_send.at[t, part],
            recv_sem=near_recv.at[t, part],
            device_id=(near, q),
            device_id_type=MESH,
        )

    def far_copy(t, part, j):
        rows = rows_in(part)
        lanes = pl.ds(j * FINE, FINE)
        return pltpu.make_async_remote_copy(
            src_ref=xbuf.at[t, SELF, rows, lanes],
            dst_ref=xbuf.at[t, FAR, rows, lanes],
            send_sem=far_send.at[t, part, j],
            recv_sem=far_recv.at[t, part, j],
            device_id=(far, q),
            device_id_type=MESH,
        )

    def send_in(phase, part):
        for i in devices_in(part):
            n, lanes = i // 2, slice((i % 2) * HALF, (i % 2 + 1) * HALF)
            a, b, c = n * 2 * PART, n * 2 * PART + PART, (n + 1) * 2 * PART
            pack(v[a:b, lanes], v[b:c, lanes], qin.at[phase, i])

            @pl.when(g != i)
            def _():
                in_copy(phase, i).start()

            @pl.when(g == i)
            def _():
                rin[phase, i] = qin[phase, i]

    def send_far(t, part, j):
        @pl.when(has_far)
        def _():
            far_copy(t, part, j).start()

    start_load.wait()
    lane = lax.broadcasted_iota(jnp.int32, (COLS, CH), 1)
    live = jnp.where(lane < counts[0], 1.0, 0.0).astype(F32)
    for j in range(CH // TILE):
        cols = slice(j * TILE, (j + 1) * TILE)
        v[:, cols] = start_v[cols, :].T * live[:, cols]
    pl.semaphore_wait(barrier, jnp.where(has_far, GROUP + 1, GROUP))
    for part in range(len(PARTS)):
        send_in(0, part)

    for load in small_loads:
        load.wait()
    mat_load.wait()
    m0, m1 = mat_v[0], mat_v[1]
    for r, (x, y) in enumerate(((m0, -m1), (m1, m0))):
        for c, part in enumerate((x, y)):
            high, low = split(part)
            bhigh[r * 128 : (r + 1) * 128, c * 128 : (c + 1) * 128] = high
            blow[r * 128 : (r + 1) * 128, c * 128 : (c + 1) * 128] = low
    pot = jnp.broadcast_to(potential[pl.ds(e, 1), :], (TILE, TILE)).T
    for j in range(HALF // TILE):
        lanes = pl.ds(pl.multiple_of((g % 2) * HALF + j * TILE, TILE), TILE)
        angle = energy[:, lanes] + pot
        cosine[:, j * TILE : (j + 1) * TILE] = jnp.cos(angle)
        sine[:, j * TILE : (j + 1) * TILE] = jnp.sin(angle)
    for l in range(ORDERS):
        rad_t[l] = jnp.concatenate([jnp.broadcast_to(radial[l : l + 1, :], (TILE, PART)).T] * (COLS // PART), axis=0)

    @pl.when(jnp.logical_not(has_far))
    def _():
        for t in range(TERMS):
            xbuf[t, FAR] = jnp.zeros((COLS, CH), BF16)

    def turn_weights(first, last):
        def body(i, _):
            l = i // 3
            k = i % 3
            pltpu.make_async_copy(coupling.at[i], raw.at[i], w_sem.at[i]).wait()
            for a in range(CH // TILE):
                for b in range(CH // TILE):
                    keep = jnp.full((TILE, TILE), pattern[a, k, 0, b].astype(F32), F32).astype(BF16)
                    tile = raw[i, a * TILE : (a + 1) * TILE, b * TILE : (b + 1) * TILE]
                    wt[
                        k,
                        b * TILE : (b + 1) * TILE,
                        pl.ds(pl.multiple_of(l * CH + a * TILE, TILE), TILE),
                    ] = tile.T * keep
            return 0

        lax.fori_loop(first, last, body, 0)

    def element(re, im):
        xhigh, xlow = split(jnp.concatenate((re, im), axis=0))
        y = jnp.dot(bhigh[...], xhigh, preferred_element_type=F32)
        y = y + jnp.dot(bhigh[...], xlow, preferred_element_type=F32)
        y = y + jnp.dot(blow[...], xhigh, preferred_element_type=F32)
        return y[:128], y[128:]

    def turn(re, im):
        c, n = cosine[...], sine[...]
        return re * c + im * n, im * c - re * n

    def radial_phase(phase):
        for i in range(GROUP):
            wait_block(in_recv.at[phase, i], rin.at[phase, i], i)
        blocks = [unpack(rin.at[phase, i]) for i in range(GROUP)]
        re = jnp.concatenate([b[0] for b in blocks], axis=0)
        im = jnp.concatenate([b[1] for b in blocks], axis=0)
        re, im = element(*turn(re, im))
        if phase == 1:
            re, im = element(*turn(re, im))
        for i in range(GROUP):
            rows = slice(i * PART, (i + 1) * PART)
            if phase < 2:
                hout[phase, i, :PART] = re[rows].astype(BF16)
                hout[phase, i, PART:] = im[rows].astype(BF16)

                @pl.when(has_far)
                def _():
                    direct_copy(phase, i).start()

            pack(re[rows], im[rows], qout.at[phase, i])

            @pl.when(g != i)
            def _():
                out_copy(phase, i).start()

            @pl.when(g == i)
            def _():
                rback[phase, i] = qout[phase, i]

    def wait_back(phase, part):
        for i in devices_in(part):
            wait_block(out_recv.at[phase, i], rback.at[phase, i], i)
            n, lanes = i // 2, slice((i % 2) * HALF, (i % 2 + 1) * HALF)
            a, b, c = n * 2 * PART, n * 2 * PART + PART, (n + 1) * 2 * PART
            v[a:b, lanes], v[b:c, lanes] = unpack(rback.at[phase, i])

    def wait_far(t, part):
        @pl.when(has_far)
        def _():
            if t % 3 == 0:
                for i in devices_in(part):
                    ref = hout.at[t // 3, i]
                    pltpu.make_async_copy(ref, ref, direct_recv.at[t // 3, i]).wait()
            else:
                for j in range(CH // FINE):
                    far_copy(t, part, j).wait_recv()

    def term(t, scale, emit, after):
        acc[...] = jnp.dot(xbuf[t, SELF], wt[1], preferred_element_type=F32)
        for part in range(len(PARTS)):
            near_copy(t, part).wait_recv()
        acc[...] += jnp.dot(xbuf[t, NEAR], wt[k_near], preferred_element_type=F32)
        for part in range(len(PARTS)):
            rows = slice(PARTS[part][0] * 2 * PART, PARTS[part][1] * 2 * PART)
            count = rows.stop - rows.start
            wait_far(t, part)
            for j in range(CH // FINE):
                total = None
                for l in range(ORDERS):
                    lanes = slice(l * CH + j * FINE, l * CH + (j + 1) * FINE)
                    y = acc[rows, lanes] + jnp.dot(
                        xbuf[t, FAR, rows, :], wt[k_far, :, lanes], preferred_element_type=F32
                    )
                    factor = jnp.concatenate((rad_t[l, :count], rad_t[l, :count]), axis=1)
                    total = y * factor if total is None else total + y * factor
                lane = lax.broadcasted_iota(jnp.int32, (count, FINE), 1) + j * FINE
                lanes = slice(j * FINE, (j + 1) * FINE)
                emit(part, rows, j, lanes, jnp.where(lane < counts[0], total * scale, 0.0))
            after(part)

    def coupling_step(step):
        base = 3 * step
        for part in range(len(PARTS)):
            wait_back(step, part)
            rows = rows_in(part)
            xbuf[base, SELF, rows] = v[rows].astype(BF16)
            near_copy(base, part).start()

        def first(part, rows, j, lanes, u):
            odd[rows, lanes] = u
            xbuf[base + 1, SELF, rows, lanes] = u.astype(BF16)
            send_far(base + 1, part, j)

        def second(part, rows, j, lanes, u):
            even[rows, lanes] = v[rows, lanes] - u
            xbuf[base + 2, SELF, rows, lanes] = u.astype(BF16)
            send_far(base + 2, part, j)

        def third(part, rows, j, lanes, u):
            o = odd[rows, lanes] - u
            ev = even[rows, lanes]
            for n in range(u.shape[0] // (2 * PART)):
                a, b, c = n * 2 * PART, n * 2 * PART + PART, (n + 1) * 2 * PART
                v[rows.start + a : rows.start + b, lanes] = ev[a:b] + o[b:c]
                v[rows.start + b : rows.start + c, lanes] = ev[b:c] - o[a:b]

        term(base, STEP, first, lambda part: near_copy(base + 1, part).start())
        term(base + 1, STEP / 2.0, second, lambda part: near_copy(base + 2, part).start())
        term(base + 2, STEP / 3.0, third, lambda part: send_in(step + 1, part))

    turn_weights(0, 5)
    radial_phase(0)
    turn_weights(5, 9)
    coupling_step(0)
    radial_phase(1)
    coupling_step(1)
    radial_phase(2)
    for part in range(len(PARTS)):
        wait_back(2, part)
    for j in range(CH // TILE):
        cols = slice(j * TILE, (j + 1) * TILE)
        out[cols, :] = v[:, cols].T

    for phase in range(PHASES):
        for i in range(GROUP):

            @pl.when(g != i)
            def _():
                in_copy(phase, i).wait_send()
                out_copy(phase, i).wait_send()

    for t in range(TERMS):
        for part in range(len(PARTS)):
            near_copy(t, part).wait_send()

    @pl.when(has_far)
    def _():
        for step in range(2):
            for i in range(GROUP):
                direct_copy(step, i).wait_send()
        for t in range(TERMS):
            if t % 3:
                for part in range(len(PARTS)):
                    for j in range(CH // FINE):
                        far_copy(t, part, j).wait_send()


def shards(
    start_amplitudes, coupling, block_pattern, counts, radial_terms, energy, potential, element_matrices
):
    start = start_amplitudes.reshape(CH, COLS)
    weights = coupling[0].transpose(0, 2, 1, 3).reshape(9, CH, CH)
    vmem = pl.BlockSpec(memory_space=pltpu.VMEM)
    smem = pl.BlockSpec(memory_space=pltpu.SMEM)
    anywhere = pl.BlockSpec(memory_space=pltpu.HBM)
    dma = pltpu.SemaphoreType.DMA
    out = pl.pallas_call(
        kernel,
        out_shape=jax.ShapeDtypeStruct((CH, COLS), F32),
        in_specs=[smem] + [anywhere] * 7,
        out_specs=vmem,
        scratch_shapes=[
            pltpu.VMEM((9, CH, CH), BF16),
            pltpu.VMEM((3, CH, ORDERS * CH), BF16),
            pltpu.VMEM((TERMS, 3, COLS, CH), BF16),
            pltpu.VMEM((2, GROUP, 2 * PART, HALF), BF16),
            pltpu.VMEM((PHASES, GROUP, BLOCK, PART, TILE), jnp.int16),
            pltpu.VMEM((PHASES, GROUP, BLOCK, PART, TILE), jnp.int16),
            pltpu.VMEM((PHASES, GROUP, BLOCK, PART, TILE), jnp.int16),
            pltpu.VMEM((PHASES, GROUP, BLOCK, PART, TILE), jnp.int16),
            pltpu.VMEM((COLS, CH), F32),
            pltpu.VMEM((COLS, ORDERS * CH), F32),
            pltpu.VMEM((COLS, CH), F32),
            pltpu.VMEM((COLS, CH), F32),
            pltpu.VMEM((TILE, HALF), F32),
            pltpu.VMEM((TILE, HALF), F32),
            pltpu.VMEM((CH, COLS), F32),
            pltpu.VMEM((2, TILE, TILE), F32),
            pltpu.VMEM((2 * TILE, 2 * TILE), BF16),
            pltpu.VMEM((2 * TILE, 2 * TILE), BF16),
            pltpu.VMEM((ORDERS, TILE, TILE), F32),
            pltpu.SMEM((6, 3, 1, 6), jnp.int32),
            pltpu.VMEM((3, PART), F32),
            pltpu.VMEM((1, CH), F32),
            pltpu.VMEM((4, TILE), F32),
            dma((6,)),
            dma((9,)),
            dma((PHASES, GROUP)),
            dma((PHASES, GROUP)),
            dma((PHASES, GROUP)),
            dma((PHASES, GROUP)),
            dma((TERMS, len(PARTS))),
            dma((TERMS, len(PARTS))),
            dma((TERMS, len(PARTS), CH // FINE)),
            dma((TERMS, len(PARTS), CH // FINE)),
            dma((2, GROUP)),
            dma((2, GROUP)),
        ],
        compiler_params=pltpu.CompilerParams(
            collective_id=0, has_side_effects=True, vmem_limit_bytes=60 * 2**20
        ),
    )(
        counts,
        block_pattern.transpose(1, 2, 0, 3),
        start,
        weights,
        radial_terms,
        energy,
        potential.reshape(4, TILE),
        element_matrices,
    )
    return out.reshape(1, CH, 1, COLS)


def solution(mesh):
    return jax.shard_map(
        shards,
        mesh=mesh,
        in_specs=(
            P("sym", None, "rad", None),
            P("sym", None, None, None, None),
            P("sym", None, None, None),
            P("sym"),
            P(None, "rad"),
            P("sym", None),
            P(),
            P(),
        ),
        out_specs=P("sym", None, "rad", None),
        check_vma=False,
    )
```

```python
import math

import jax
import jax.numpy as jnp
from jax import lax
from jax.experimental import pallas as pl
from jax.experimental.pallas import tpu as pltpu
from jax.sharding import PartitionSpec as P

MESH = pl.DeviceIdType.MESH
STEP = 0.8
CH = 768
COLS = 128
HALF = CH // 2
PART = 16
GROUP = 8
ORDERS = 3
TILE = 128
FINE = 256
TERMS = 6
PHASES = 3
SELF, NEAR, FAR = 0, 1, 2
BLOCK = 7
LEVELS = 64.0
FULL = 32760.0
PARTS = 2
ROWS = COLS // PARTS
STATES = ROWS // (2 * PART)
BLOCKS = GROUP // PARTS
F32 = jnp.float32
BF16 = jnp.bfloat16


def split(x):
    high = x.astype(BF16)
    return high, (x - high.astype(F32)).astype(BF16)


def pack(re, im, ref):
    rows = lax.broadcasted_iota(jnp.int32, (PART, TILE), 0)
    scales = jnp.zeros((PART, TILE), F32)
    for c in range(HALF // TILE):
        lanes = slice(c * TILE, (c + 1) * TILE)
        a, b = re[:, lanes], im[:, lanes]
        top = jnp.max(jnp.maximum(jnp.abs(a), jnp.abs(b)), axis=0, keepdims=True)
        level = jnp.ceil(jnp.log(jnp.maximum(top, 1e-36)) * (LEVELS / math.log(2.0)))
        factor = jnp.exp2(level * (-1.0 / LEVELS))
        ref[c] = jnp.round(a * factor * FULL).astype(jnp.int32).astype(jnp.int16)
        ref[3 + c] = jnp.round(b * factor * FULL).astype(jnp.int32).astype(jnp.int16)
        scales = jnp.where(rows == c, level, scales)
    ref[6] = scales.astype(jnp.int32).astype(jnp.int16)


def unpack(ref):
    level = ref[6].astype(jnp.int32).astype(F32)
    factor = jnp.exp2(level * (1.0 / LEVELS)) * (1.0 / FULL)
    parts = []
    for first in (0, 3):
        tiles = [
            ref[first + c].astype(jnp.int32).astype(F32) * factor[c : c + 1] for c in range(HALF // TILE)
        ]
        parts.append(jnp.concatenate(tiles, axis=1))
    return parts


def kernel(
    counts, pattern_h, start, coupling, radial_h, energy_h, potential_h, matrices,
    out,
    raw, wt, xbuf, hout, qin, rin, qout, rback, v, acc, odd, turned, cosine, sine, start_v, mat_v, bhigh, blow, rad_t,
    pattern, radial, energy, potential, load_sem, w_sem, in_send, in_recv, out_send, out_recv, near_send, near_recv,
    far_send, far_recv, direct_send, direct_recv,
):
    s = lax.axis_index("sym")
    q = lax.axis_index("rad")
    e = q // GROUP
    g = q % GROUP
    above_near = s % 2 == 0
    near = jnp.where(above_near, s + 1, s - 1)
    far = jnp.where(above_near, s - 1, s + 1)
    has_far = jnp.logical_and(far >= 0, far < 8)
    k_near = jnp.where(above_near, 2, 0)
    k_far = jnp.where(above_near, 0, 2)

    start_load = pltpu.make_async_copy(start, start_v, load_sem.at[0])
    start_load.start()
    mat_load = pltpu.make_async_copy(matrices.at[:, e], mat_v, load_sem.at[1])
    mat_load.start()
    small_loads = [
        pltpu.make_async_copy(a, b, load_sem.at[2 + i])
        for i, (a, b) in enumerate(
            ((energy_h, energy), (potential_h, potential), (radial_h, radial), (pattern_h, pattern))
        )
    ]
    for load in small_loads:
        load.start()
    w_loads = [pltpu.make_async_copy(coupling.at[i], raw.at[i], w_sem.at[i]) for i in range(9)]
    for load in w_loads:
        load.start()

    barrier = pltpu.get_barrier_semaphore()
    for d in range(1, GROUP):
        pl.semaphore_signal(
            barrier, inc=1, device_id=(s, e * GROUP + (g + d) % GROUP), device_id_type=MESH
        )
    pl.semaphore_signal(barrier, inc=1, device_id=(near, q), device_id_type=MESH)

    @pl.when(has_far)
    def _():
        pl.semaphore_signal(barrier, inc=1, device_id=(far, q), device_id_type=MESH)

    def in_copy(phase, i):
        return pltpu.make_async_remote_copy(
            src_ref=qin.at[phase, i],
            dst_ref=rin.at[phase, g],
            send_sem=in_send.at[phase, i],
            recv_sem=in_recv.at[phase, g],
            device_id=(s, e * GROUP + i),
            device_id_type=MESH,
        )

    def out_copy(phase, i):
        return pltpu.make_async_remote_copy(
            src_ref=qout.at[phase, i],
            dst_ref=rback.at[phase, g],
            send_sem=out_send.at[phase, i],
            recv_sem=out_recv.at[phase, g],
            device_id=(s, e * GROUP + i),
            device_id_type=MESH,
        )

    def wait_block(recv_sem, ref, i):
        @pl.when(g != i)
        def _():
            pltpu.make_async_copy(ref, ref, recv_sem).wait()

    def rows_of(i):
        return pl.ds(pl.multiple_of((i // 2) * 2 * PART, 2 * PART), 2 * PART)

    def lanes_of(i):
        return pl.ds(pl.multiple_of((i % 2) * HALF, HALF), HALF)

    def direct_copy(step, i):
        return pltpu.make_async_remote_copy(
            src_ref=hout.at[step, i],
            dst_ref=xbuf.at[3 * step, FAR, rows_of(g), lanes_of(g)],
            send_sem=direct_send.at[step, i],
            recv_sem=direct_recv.at[step, g],
            device_id=(far, e * GROUP + i),
            device_id_type=MESH,
        )

    def rows_in(part):
        return pl.ds(pl.multiple_of(part * ROWS, ROWS), ROWS)

    def near_copy(t, part):
        rows = rows_in(part)
        return pltpu.make_async_remote_copy(
            src_ref=xbuf.at[t, SELF, rows],
            dst_ref=xbuf.at[t, NEAR, rows],
            send_sem=near_send.at[t, part],
            recv_sem=near_recv.at[t, part],
            device_id=(near, q),
            device_id_type=MESH,
        )

    def far_copy(t, part):
        rows = rows_in(part)
        return pltpu.make_async_remote_copy(
            src_ref=xbuf.at[t, SELF, rows],
            dst_ref=xbuf.at[t, FAR, rows],
            send_sem=far_send.at[t, part],
            recv_sem=far_recv.at[t, part],
            device_id=(far, q),
            device_id_type=MESH,
        )

    def block_at(part, b):
        first = pl.multiple_of(part * ROWS, ROWS) + (b // 2) * 2 * PART
        lanes = slice((b % 2) * HALF, (b % 2 + 1) * HALF)
        real = pl.ds(pl.multiple_of(first, PART), PART)
        imag = pl.ds(pl.multiple_of(first + PART, PART), PART)
        return part * BLOCKS + b, real, imag, lanes

    def send_in(phase, part):
        for b in range(BLOCKS):
            i, real, imag, lanes = block_at(part, b)
            pack(
                v[real, lanes] + odd[imag, lanes],
                v[imag, lanes] - odd[real, lanes],
                qin.at[phase, i],
            )

            @pl.when(g != i)
            def _():
                in_copy(phase, i).start()

            @pl.when(g == i)
            def _():
                rin[phase, i] = qin[phase, i]

    start_load.wait()
    lane = lax.broadcasted_iota(jnp.int32, (COLS, CH), 1)
    live = jnp.where(lane < counts[0], 1.0, 0.0).astype(F32)
    for j in range(CH // TILE):
        cols = slice(j * TILE, (j + 1) * TILE)
        v[:, cols] = start_v[cols, :].T * live[:, cols]
    pl.semaphore_wait(barrier, jnp.where(has_far, GROUP + 1, GROUP))
    odd[...] = jnp.zeros_like(odd)

    def send_first(part, _):
        send_in(0, part)
        return 0

    lax.fori_loop(0, PARTS, send_first, 0)

    for load in small_loads:
        load.wait()
    mat_load.wait()
    m0, m1 = mat_v[0], mat_v[1]
    for r, (x, y) in enumerate(((m0, -m1), (m1, m0))):
        for c, part in enumerate((x, y)):
            high, low = split(part)
            bhigh[r * 128 : (r + 1) * 128, c * 128 : (c + 1) * 128] = high
            blow[r * 128 : (r + 1) * 128, c * 128 : (c + 1) * 128] = low
    pot = jnp.broadcast_to(potential[pl.ds(e, 1), :], (TILE, TILE)).T
    for j in range(HALF // TILE):
        lanes = pl.ds(pl.multiple_of((g % 2) * HALF + j * TILE, TILE), TILE)
        angle = energy[:, lanes] + pot
        cosine[:, j * TILE : (j + 1) * TILE] = jnp.cos(angle)
        sine[:, j * TILE : (j + 1) * TILE] = jnp.sin(angle)
    for l in range(ORDERS):
        rad_t[l] = jnp.concatenate([jnp.broadcast_to(radial[l : l + 1, :], (TILE, PART)).T] * (COLS // PART), axis=0)

    @pl.when(jnp.logical_not(has_far))
    def _():
        def clear(t, _):
            xbuf[t, FAR] = jnp.zeros((COLS, CH), BF16)
            return 0

        lax.fori_loop(0, TERMS, clear, 0)

    def turn_weights(first, last):
        def body(i, _):
            l = i // 3
            k = i % 3
            pltpu.make_async_copy(coupling.at[i], raw.at[i], w_sem.at[i]).wait()
            for a in range(CH // TILE):
                for b in range(CH // TILE):
                    keep = jnp.full((TILE, TILE), pattern[a, k, 0, b].astype(F32), F32).astype(BF16)
                    tile = raw[i, a * TILE : (a + 1) * TILE, b * TILE : (b + 1) * TILE]
                    wt[
                        k,
                        b * TILE : (b + 1) * TILE,
                        pl.ds(pl.multiple_of(l * CH + a * TILE, TILE), TILE),
                    ] = tile.T * keep
            return 0

        lax.fori_loop(first, last, body, 0)

    def radial_step(_, carry):
        re, im = turned[:128], turned[128:]
        c, n = cosine[...], sine[...]
        xhigh, xlow = split(jnp.concatenate((re * c + im * n, im * c - re * n), axis=0))
        y = jnp.dot(bhigh[...], xhigh, preferred_element_type=F32)
        y = y + jnp.dot(bhigh[...], xlow, preferred_element_type=F32)
        turned[...] = y + jnp.dot(blow[...], xhigh, preferred_element_type=F32)
        return carry

    def radial_phase(phase):
        for i in range(GROUP):
            wait_block(in_recv.at[phase, i], rin.at[phase, i], i)
        for i in range(GROUP):
            rows = slice(i * PART, (i + 1) * PART)
            turned[i * PART : (i + 1) * PART], turned[128 + i * PART : 128 + (i + 1) * PART] = unpack(
                rin.at[phase, i]
            )
        lax.fori_loop(0, jnp.where(phase == 1, 2, 1), radial_step, 0)
        for i in range(GROUP):
            re = turned[i * PART : (i + 1) * PART]
            im = turned[128 + i * PART : 128 + (i + 1) * PART]
            hout[phase, i, :PART] = re.astype(BF16)
            hout[phase, i, PART:] = im.astype(BF16)
            pack(re, im, qout.at[phase, i])

        def send(i, _):
            @pl.when(jnp.logical_and(has_far, phase < 2))
            def _():
                direct_copy(phase, i).start()

            @pl.when(g != i)
            def _():
                out_copy(phase, i).start()

            @pl.when(g == i)
            def _():
                rback[phase, i] = qout[phase, i]

            return 0

        lax.fori_loop(0, GROUP, send, 0)

    def back(phase):
        def body(part, _):
            for b in range(BLOCKS):
                i, real, imag, lanes = block_at(part, b)
                wait_block(out_recv.at[phase, i], rback.at[phase, i], i)
            for b in range(BLOCKS):
                i, real, imag, lanes = block_at(part, b)
                v[real, lanes], v[imag, lanes] = unpack(rback.at[phase, i])
            rows = rows_in(part)
            xbuf[3 * phase, SELF, rows] = v[rows].astype(BF16)

            @pl.when(phase < 2)
            def _():
                near_copy(3 * phase, part).start()

            return 0

        lax.fori_loop(0, PARTS, body, 0)

    def wait_far(phase, order, part):
        @pl.when(jnp.logical_and(has_far, order == 0))
        def _():
            for b in range(BLOCKS):
                i = part * BLOCKS + b
                ref = hout.at[phase, i]
                pltpu.make_async_copy(ref, ref, direct_recv.at[phase, i]).wait()

        @pl.when(jnp.logical_and(has_far, order > 0))
        def _():
            far_copy(3 * phase + order, part).wait_recv()

    def term(phase, order):
        t = 3 * phase + order
        scale = jnp.where(order == 0, STEP, jnp.where(order == 1, STEP / 2.0, STEP / 3.0))
        keep_odd = jnp.where(order == 0, 0.0, 1.0)
        add_odd = jnp.where(order == 0, 1.0, jnp.where(order == 1, 0.0, -1.0))
        add_even = jnp.where(order == 1, -1.0, 0.0)
        acc[...] = jnp.dot(xbuf[t, SELF], wt[1], preferred_element_type=F32)
        for part in range(PARTS):
            near_copy(t, part).wait_recv()
        acc[...] += jnp.dot(xbuf[t, NEAR], wt[k_near], preferred_element_type=F32)

        def body(part, _):
            rows = rows_in(part)
            wait_far(phase, order, part)
            for j in range(CH // FINE):
                total = None
                for l in range(ORDERS):
                    lanes = slice(l * CH + j * FINE, l * CH + (j + 1) * FINE)
                    y = acc[rows, lanes] + jnp.dot(
                        xbuf[t, FAR, rows, :], wt[k_far, :, lanes], preferred_element_type=F32
                    )
                    factor = jnp.concatenate((rad_t[l, :ROWS], rad_t[l, :ROWS]), axis=1)
                    total = y * factor if total is None else total + y * factor
                lane = lax.broadcasted_iota(jnp.int32, (ROWS, FINE), 1) + j * FINE
                lanes = slice(j * FINE, (j + 1) * FINE)
                u = jnp.where(lane < counts[0], total * scale, 0.0)
                odd[rows, lanes] = odd[rows, lanes] * keep_odd + u * add_odd
                v[rows, lanes] += u * add_even
                xbuf[t + 1, SELF, rows, lanes] = u.astype(BF16)

            @pl.when(jnp.logical_and(has_far, order < 2))
            def _():
                far_copy(t + 1, part).start()

            @pl.when(order < 2)
            def _():
                near_copy(t + 1, part).start()

            @pl.when(order == 2)
            def _():
                send_in(phase + 1, part)

            return 0

        lax.fori_loop(0, PARTS, body, 0)

    turn_weights(0, 5)

    def one_phase(phase, _):
        radial_phase(phase)

        @pl.when(phase == 0)
        def _():
            turn_weights(5, 9)

        back(phase)

        @pl.when(phase < 2)
        def _():
            def body(order, _):
                term(phase, order)
                return 0

            lax.fori_loop(0, 3, body, 0)

        return 0

    lax.fori_loop(0, PHASES, one_phase, 0)
    for j in range(CH // TILE):
        cols = slice(j * TILE, (j + 1) * TILE)
        out[cols, :] = v[:, cols].T

    def end_phase(phase, _):
        def body(i, _):
            @pl.when(g != i)
            def _():
                in_copy(phase, i).wait_send()
                out_copy(phase, i).wait_send()

            @pl.when(jnp.logical_and(has_far, phase < 2))
            def _():
                direct_copy(phase, i).wait_send()

            return 0

        return lax.fori_loop(0, GROUP, body, 0)

    lax.fori_loop(0, PHASES, end_phase, 0)

    def end_term(t, _):
        for part in range(PARTS):
            near_copy(t, part).wait_send()

            @pl.when(jnp.logical_and(has_far, t % 3 > 0))
            def _():
                far_copy(t, part).wait_send()

        return 0

    lax.fori_loop(0, TERMS, end_term, 0)


def shards(
    start_amplitudes, coupling, block_pattern, counts, radial_terms, energy, potential, element_matrices
):
    start = start_amplitudes.reshape(CH, COLS)
    weights = coupling[0].transpose(0, 2, 1, 3).reshape(9, CH, CH)
    vmem = pl.BlockSpec(memory_space=pltpu.VMEM)
    smem = pl.BlockSpec(memory_space=pltpu.SMEM)
    anywhere = pl.BlockSpec(memory_space=pltpu.HBM)
    dma = pltpu.SemaphoreType.DMA
    out = pl.pallas_call(
        kernel,
        out_shape=jax.ShapeDtypeStruct((CH, COLS), F32),
        in_specs=[smem] + [anywhere] * 7,
        out_specs=vmem,
        scratch_shapes=[
            pltpu.VMEM((9, CH, CH), BF16),
            pltpu.VMEM((3, CH, ORDERS * CH), BF16),
            pltpu.VMEM((TERMS + 1, 3, COLS, CH), BF16),
            pltpu.VMEM((PHASES, GROUP, 2 * PART, HALF), BF16),
            pltpu.VMEM((PHASES, GROUP, BLOCK, PART, TILE), jnp.int16),
            pltpu.VMEM((PHASES, GROUP, BLOCK, PART, TILE), jnp.int16),
            pltpu.VMEM((PHASES, GROUP, BLOCK, PART, TILE), jnp.int16),
            pltpu.VMEM((PHASES, GROUP, BLOCK, PART, TILE), jnp.int16),
            pltpu.VMEM((COLS, CH), F32),
            pltpu.VMEM((COLS, ORDERS * CH), F32),
            pltpu.VMEM((COLS, CH), F32),
            pltpu.VMEM((2 * TILE, HALF), F32),
            pltpu.VMEM((TILE, HALF), F32),
            pltpu.VMEM((TILE, HALF), F32),
            pltpu.VMEM((CH, COLS), F32),
            pltpu.VMEM((2, TILE, TILE), F32),
            pltpu.VMEM((2 * TILE, 2 * TILE), BF16),
            pltpu.VMEM((2 * TILE, 2 * TILE), BF16),
            pltpu.VMEM((ORDERS, TILE, TILE), F32),
            pltpu.SMEM((6, 3, 1, 6), jnp.int32),
            pltpu.VMEM((3, PART), F32),
            pltpu.VMEM((1, CH), F32),
            pltpu.VMEM((4, TILE), F32),
            dma((6,)),
            dma((9,)),
            dma((PHASES, GROUP)),
            dma((PHASES, GROUP)),
            dma((PHASES, GROUP)),
            dma((PHASES, GROUP)),
            dma((TERMS, PARTS)),
            dma((TERMS, PARTS)),
            dma((TERMS, PARTS)),
            dma((TERMS, PARTS)),
            dma((2, GROUP)),
            dma((2, GROUP)),
        ],
        compiler_params=pltpu.CompilerParams(
            collective_id=0, has_side_effects=True, vmem_limit_bytes=60 * 2**20
        ),
    )(
        counts,
        block_pattern.transpose(1, 2, 0, 3),
        start,
        weights,
        radial_terms,
        energy,
        potential.reshape(4, TILE),
        element_matrices,
    )
    return out.reshape(1, CH, 1, COLS)


def solution(mesh):
    return jax.shard_map(
        shards,
        mesh=mesh,
        in_specs=(
            P("sym", None, "rad", None),
            P("sym", None, None, None, None),
            P("sym", None, None, None),
            P("sym"),
            P(None, "rad"),
            P("sym", None),
            P(),
            P(),
        ),
        out_specs=P("sym", None, "rad", None),
        check_vma=False,
    )
```

```python
import math

import jax
import jax.numpy as jnp
from jax import lax
from jax.experimental import pallas as pl
from jax.experimental.pallas import tpu as pltpu
from jax.sharding import PartitionSpec as P

MESH = pl.DeviceIdType.MESH
STEP = 0.8
CH = 768
COLS = 128
HALF = CH // 2
PART = 16
GROUP = 8
ORDERS = 3
TILE = 128
FINE = 256
TERMS = 6
PHASES = 3
SELF, NEAR, FAR = 0, 1, 2
BLOCK = 7
LEVELS = 64.0
FULL = 32760.0
PARTS = 2
ROWS = COLS // PARTS
STATES = ROWS // (2 * PART)
BLOCKS = GROUP // PARTS
F32 = jnp.float32
BF16 = jnp.bfloat16


def split(x):
    high = x.astype(BF16)
    return high, (x - high.astype(F32)).astype(BF16)


def pack(re, im, ref):
    rows = lax.broadcasted_iota(jnp.int32, (PART, TILE), 0)
    scales = jnp.zeros((PART, TILE), F32)
    for c in range(HALF // TILE):
        lanes = slice(c * TILE, (c + 1) * TILE)
        a, b = re[:, lanes], im[:, lanes]
        top = jnp.max(jnp.maximum(jnp.abs(a), jnp.abs(b)), axis=0, keepdims=True)
        level = jnp.ceil(jnp.log(jnp.maximum(top, 1e-36)) * (LEVELS / math.log(2.0)))
        factor = jnp.exp2(level * (-1.0 / LEVELS))
        ref[c] = jnp.round(a * factor * FULL).astype(jnp.int32).astype(jnp.int16)
        ref[3 + c] = jnp.round(b * factor * FULL).astype(jnp.int32).astype(jnp.int16)
        scales = jnp.where(rows == c, level, scales)
    ref[6] = scales.astype(jnp.int32).astype(jnp.int16)


def unpack(ref):
    level = ref[6].astype(jnp.int32).astype(F32)
    factor = jnp.exp2(level * (1.0 / LEVELS)) * (1.0 / FULL)
    parts = []
    for first in (0, 3):
        tiles = [
            ref[first + c].astype(jnp.int32).astype(F32) * factor[c : c + 1] for c in range(HALF // TILE)
        ]
        parts.append(jnp.concatenate(tiles, axis=1))
    return parts


def kernel(
    counts, pattern_h, start, coupling, radial_h, energy_h, potential_h, matrices,
    out,
    raw, wt, xbuf, hout, qin, rin, qout, rback, v, acc, odd, turned, cosine, sine, start_v, mat_v, bhigh, blow, rad_t,
    pattern, radial, energy, potential, load_sem, w_sem, in_send, in_recv, out_send, out_recv, near_send, near_recv,
    far_send, far_recv, direct_send, direct_recv,
):
    s = lax.axis_index("sym")
    q = lax.axis_index("rad")
    e = q // GROUP
    g = q % GROUP
    above_near = s % 2 == 0
    near = jnp.where(above_near, s + 1, s - 1)
    far = jnp.where(above_near, s - 1, s + 1)
    has_far = jnp.logical_and(far >= 0, far < 8)
    k_near = jnp.where(above_near, 2, 0)
    k_far = jnp.where(above_near, 0, 2)

    start_load = pltpu.make_async_copy(start, start_v, load_sem.at[0])
    start_load.start()
    mat_load = pltpu.make_async_copy(matrices.at[:, e], mat_v, load_sem.at[1])
    mat_load.start()
    small_loads = [
        pltpu.make_async_copy(a, b, load_sem.at[2 + i])
        for i, (a, b) in enumerate(
            ((energy_h, energy), (potential_h, potential), (radial_h, radial), (pattern_h, pattern))
        )
    ]
    for load in small_loads:
        load.start()
    w_loads = [pltpu.make_async_copy(coupling.at[i], raw.at[i], w_sem.at[i]) for i in range(9)]
    for load in w_loads:
        load.start()

    barrier = pltpu.get_barrier_semaphore()
    for d in range(1, GROUP):
        pl.semaphore_signal(
            barrier, inc=1, device_id=(s, e * GROUP + (g + d) % GROUP), device_id_type=MESH
        )
    pl.semaphore_signal(barrier, inc=1, device_id=(near, q), device_id_type=MESH)

    @pl.when(has_far)
    def _():
        pl.semaphore_signal(barrier, inc=1, device_id=(far, q), device_id_type=MESH)

    def in_copy(phase, i):
        return pltpu.make_async_remote_copy(
            src_ref=qin.at[phase, i],
            dst_ref=rin.at[phase, g],
            send_sem=in_send.at[phase, i],
            recv_sem=in_recv.at[phase, g],
            device_id=(s, e * GROUP + i),
            device_id_type=MESH,
        )

    def out_copy(phase, i):
        return pltpu.make_async_remote_copy(
            src_ref=qout.at[phase, i],
            dst_ref=rback.at[phase, g],
            send_sem=out_send.at[phase, i],
            recv_sem=out_recv.at[phase, g],
            device_id=(s, e * GROUP + i),
            device_id_type=MESH,
        )

    def wait_block(recv_sem, ref, i):
        @pl.when(g != i)
        def _():
            pltpu.make_async_copy(ref, ref, recv_sem).wait()

    def rows_of(i):
        return pl.ds(pl.multiple_of((i // 2) * 2 * PART, 2 * PART), 2 * PART)

    def lanes_of(i):
        return pl.ds(pl.multiple_of((i % 2) * HALF, HALF), HALF)

    def direct_copy(step, i):
        return pltpu.make_async_remote_copy(
            src_ref=hout.at[step, i],
            dst_ref=xbuf.at[3 * step, FAR, rows_of(g), lanes_of(g)],
            send_sem=direct_send.at[step, i],
            recv_sem=direct_recv.at[step, g],
            device_id=(far, e * GROUP + i),
            device_id_type=MESH,
        )

    def rows_in(part):
        return pl.ds(pl.multiple_of(part * ROWS, ROWS), ROWS)

    def near_copy(t, part):
        rows = rows_in(part)
        return pltpu.make_async_remote_copy(
            src_ref=xbuf.at[t, SELF, rows],
            dst_ref=xbuf.at[t, NEAR, rows],
            send_sem=near_send.at[t, part],
            recv_sem=near_recv.at[t, part],
            device_id=(near, q),
            device_id_type=MESH,
        )

    def far_copy(t, part):
        rows = rows_in(part)
        return pltpu.make_async_remote_copy(
            src_ref=xbuf.at[t, SELF, rows],
            dst_ref=xbuf.at[t, FAR, rows],
            send_sem=far_send.at[t, part],
            recv_sem=far_recv.at[t, part],
            device_id=(far, q),
            device_id_type=MESH,
        )

    def block_at(part, b):
        first = pl.multiple_of(part * ROWS, ROWS) + (b // 2) * 2 * PART
        lanes = slice((b % 2) * HALF, (b % 2 + 1) * HALF)
        real = pl.ds(pl.multiple_of(first, PART), PART)
        imag = pl.ds(pl.multiple_of(first + PART, PART), PART)
        return part * BLOCKS + b, real, imag, lanes

    def send_in(phase, part):
        for b in range(BLOCKS):
            i, real, imag, lanes = block_at(part, b)
            pack(
                v[real, lanes] + odd[imag, lanes],
                v[imag, lanes] - odd[real, lanes],
                qin.at[phase, i],
            )

            @pl.when(g != i)
            def _():
                in_copy(phase, i).start()

            @pl.when(g == i)
            def _():
                rin[phase, i] = qin[phase, i]

    start_load.wait()
    lane = lax.broadcasted_iota(jnp.int32, (COLS, CH), 1)
    live = jnp.where(lane < counts[0], 1.0, 0.0).astype(F32)
    for j in range(CH // TILE):
        cols = slice(j * TILE, (j + 1) * TILE)
        v[:, cols] = start_v[cols, :].T * live[:, cols]
    pl.semaphore_wait(barrier, jnp.where(has_far, GROUP + 1, GROUP))
    odd[...] = jnp.zeros_like(odd)

    def send_first(part, _):
        send_in(0, part)
        return 0

    lax.fori_loop(0, PARTS, send_first, 0)

    for load in small_loads:
        load.wait()
    mat_load.wait()
    m0, m1 = mat_v[0], mat_v[1]
    for r, (x, y) in enumerate(((m0, -m1), (m1, m0))):
        for c, part in enumerate((x, y)):
            high, low = split(part)
            bhigh[r * 128 : (r + 1) * 128, c * 128 : (c + 1) * 128] = high
            blow[r * 128 : (r + 1) * 128, c * 128 : (c + 1) * 128] = low
    pot = jnp.broadcast_to(potential[pl.ds(e, 1), :], (TILE, TILE)).T
    for j in range(HALF // TILE):
        lanes = pl.ds(pl.multiple_of((g % 2) * HALF + j * TILE, TILE), TILE)
        angle = energy[:, lanes] + pot
        cosine[:, j * TILE : (j + 1) * TILE] = jnp.cos(angle)
        sine[:, j * TILE : (j + 1) * TILE] = jnp.sin(angle)
    for l in range(ORDERS):
        rad_t[l] = jnp.concatenate([jnp.broadcast_to(radial[l : l + 1, :], (TILE, PART)).T] * (COLS // PART), axis=0)

    @pl.when(jnp.logical_not(has_far))
    def _():
        def clear(t, _):
            xbuf[t, FAR] = jnp.zeros((COLS, CH), BF16)
            return 0

        lax.fori_loop(0, TERMS, clear, 0)

    def turn_weights(first, last):
        def body(i, _):
            l = i // 3
            k = i % 3
            pltpu.make_async_copy(coupling.at[i], raw.at[i], w_sem.at[i]).wait()
            for a in range(CH // TILE):
                for b in range(CH // TILE):
                    keep = jnp.full((TILE, TILE), pattern[a, k, 0, b].astype(F32), F32).astype(BF16)
                    tile = raw[i, a * TILE : (a + 1) * TILE, b * TILE : (b + 1) * TILE]
                    wt[
                        k,
                        b * TILE : (b + 1) * TILE,
                        pl.ds(pl.multiple_of(l * CH + a * TILE, TILE), TILE),
                    ] = tile.T * keep
            return 0

        lax.fori_loop(first, last, body, 0)

    def radial_step(_, carry):
        re, im = turned[:128], turned[128:]
        c, n = cosine[...], sine[...]
        xhigh, xlow = split(jnp.concatenate((re * c + im * n, im * c - re * n), axis=0))
        y = jnp.dot(bhigh[...], xhigh, preferred_element_type=F32)
        y = y + jnp.dot(bhigh[...], xlow, preferred_element_type=F32)
        turned[...] = y + jnp.dot(blow[...], xhigh, preferred_element_type=F32)
        return carry

    def radial_phase(phase):
        for i in range(GROUP):
            wait_block(in_recv.at[phase, i], rin.at[phase, i], i)
        for i in range(GROUP):
            rows = slice(i * PART, (i + 1) * PART)
            turned[i * PART : (i + 1) * PART], turned[128 + i * PART : 128 + (i + 1) * PART] = unpack(
                rin.at[phase, i]
            )
        lax.fori_loop(0, jnp.where(phase == 1, 2, 1), radial_step, 0)
        for i in range(GROUP):
            re = turned[i * PART : (i + 1) * PART]
            im = turned[128 + i * PART : 128 + (i + 1) * PART]
            hout[phase, i, :PART] = re.astype(BF16)
            hout[phase, i, PART:] = im.astype(BF16)

        @pl.when(jnp.logical_and(has_far, phase < 2))
        def _():
            def straight(i, _):
                direct_copy(phase, i).start()
                return 0

            lax.fori_loop(0, GROUP, straight, 0)

        for i in range(GROUP):
            re = turned[i * PART : (i + 1) * PART]
            im = turned[128 + i * PART : 128 + (i + 1) * PART]
            pack(re, im, qout.at[phase, i])

        def send(i, _):
            @pl.when(g != i)
            def _():
                out_copy(phase, i).start()

            @pl.when(g == i)
            def _():
                rback[phase, i] = qout[phase, i]

            return 0

        lax.fori_loop(0, GROUP, send, 0)

    def back(phase):
        def body(part, _):
            for b in range(BLOCKS):
                i, real, imag, lanes = block_at(part, b)
                wait_block(out_recv.at[phase, i], rback.at[phase, i], i)
            for b in range(BLOCKS):
                i, real, imag, lanes = block_at(part, b)
                v[real, lanes], v[imag, lanes] = unpack(rback.at[phase, i])
            rows = rows_in(part)
            xbuf[3 * phase, SELF, rows] = v[rows].astype(BF16)

            @pl.when(phase < 2)
            def _():
                near_copy(3 * phase, part).start()

            return 0

        lax.fori_loop(0, PARTS, body, 0)

    def wait_far(phase, order, part):
        @pl.when(jnp.logical_and(has_far, order == 0))
        def _():
            for b in range(BLOCKS):
                i = part * BLOCKS + b
                ref = hout.at[phase, i]
                pltpu.make_async_copy(ref, ref, direct_recv.at[phase, i]).wait()

        @pl.when(jnp.logical_and(has_far, order > 0))
        def _():
            far_copy(3 * phase + order, part).wait_recv()

    def term(phase, order):
        t = 3 * phase + order
        scale = jnp.where(order == 0, STEP, jnp.where(order == 1, STEP / 2.0, STEP / 3.0))
        keep_odd = jnp.where(order == 0, 0.0, 1.0)
        add_odd = jnp.where(order == 0, 1.0, jnp.where(order == 1, 0.0, -1.0))
        add_even = jnp.where(order == 1, -1.0, 0.0)
        acc[...] = jnp.dot(xbuf[t, SELF], wt[1], preferred_element_type=F32)
        for part in range(PARTS):
            near_copy(t, part).wait_recv()
        acc[...] += jnp.dot(xbuf[t, NEAR], wt[k_near], preferred_element_type=F32)

        def body(part, _):
            rows = rows_in(part)
            wait_far(phase, order, part)
            for j in range(CH // FINE):
                total = None
                for l in range(ORDERS):
                    lanes = slice(l * CH + j * FINE, l * CH + (j + 1) * FINE)
                    y = acc[rows, lanes] + jnp.dot(
                        xbuf[t, FAR, rows, :], wt[k_far, :, lanes], preferred_element_type=F32
                    )
                    factor = jnp.concatenate((rad_t[l, :ROWS], rad_t[l, :ROWS]), axis=1)
                    total = y * factor if total is None else total + y * factor
                lane = lax.broadcasted_iota(jnp.int32, (ROWS, FINE), 1) + j * FINE
                lanes = slice(j * FINE, (j + 1) * FINE)
                u = jnp.where(lane < counts[0], total * scale, 0.0)
                odd[rows, lanes] = odd[rows, lanes] * keep_odd + u * add_odd
                v[rows, lanes] += u * add_even
                xbuf[t + 1, SELF, rows, lanes] = u.astype(BF16)

            @pl.when(jnp.logical_and(has_far, order < 2))
            def _():
                far_copy(t + 1, part).start()

            @pl.when(order < 2)
            def _():
                near_copy(t + 1, part).start()

            @pl.when(order == 2)
            def _():
                send_in(phase + 1, part)

            return 0

        lax.fori_loop(0, PARTS, body, 0)

    turn_weights(0, 5)

    def one_phase(phase, _):
        radial_phase(phase)

        @pl.when(phase == 0)
        def _():
            turn_weights(5, 9)

        back(phase)

        @pl.when(phase < 2)
        def _():
            def body(order, _):
                term(phase, order)
                return 0

            lax.fori_loop(0, 3, body, 0)

        return 0

    lax.fori_loop(0, PHASES, one_phase, 0)
    for j in range(CH // TILE):
        cols = slice(j * TILE, (j + 1) * TILE)
        out[cols, :] = v[:, cols].T

    def end_phase(phase, _):
        def body(i, _):
            @pl.when(g != i)
            def _():
                in_copy(phase, i).wait_send()
                out_copy(phase, i).wait_send()

            @pl.when(jnp.logical_and(has_far, phase < 2))
            def _():
                direct_copy(phase, i).wait_send()

            return 0

        return lax.fori_loop(0, GROUP, body, 0)

    lax.fori_loop(0, PHASES, end_phase, 0)

    def end_term(t, _):
        for part in range(PARTS):
            near_copy(t, part).wait_send()

            @pl.when(jnp.logical_and(has_far, t % 3 > 0))
            def _():
                far_copy(t, part).wait_send()

        return 0

    lax.fori_loop(0, TERMS, end_term, 0)


def shards(
    start_amplitudes, coupling, block_pattern, counts, radial_terms, energy, potential, element_matrices
):
    start = start_amplitudes.reshape(CH, COLS)
    weights = coupling[0].transpose(0, 2, 1, 3).reshape(9, CH, CH)
    vmem = pl.BlockSpec(memory_space=pltpu.VMEM)
    smem = pl.BlockSpec(memory_space=pltpu.SMEM)
    anywhere = pl.BlockSpec(memory_space=pltpu.HBM)
    dma = pltpu.SemaphoreType.DMA
    out = pl.pallas_call(
        kernel,
        out_shape=jax.ShapeDtypeStruct((CH, COLS), F32),
        in_specs=[smem] + [anywhere] * 7,
        out_specs=vmem,
        scratch_shapes=[
            pltpu.VMEM((9, CH, CH), BF16),
            pltpu.VMEM((3, CH, ORDERS * CH), BF16),
            pltpu.VMEM((TERMS + 1, 3, COLS, CH), BF16),
            pltpu.VMEM((PHASES, GROUP, 2 * PART, HALF), BF16),
            pltpu.VMEM((PHASES, GROUP, BLOCK, PART, TILE), jnp.int16),
            pltpu.VMEM((PHASES, GROUP, BLOCK, PART, TILE), jnp.int16),
            pltpu.VMEM((PHASES, GROUP, BLOCK, PART, TILE), jnp.int16),
            pltpu.VMEM((PHASES, GROUP, BLOCK, PART, TILE), jnp.int16),
            pltpu.VMEM((COLS, CH), F32),
            pltpu.VMEM((COLS, ORDERS * CH), F32),
            pltpu.VMEM((COLS, CH), F32),
            pltpu.VMEM((2 * TILE, HALF), F32),
            pltpu.VMEM((TILE, HALF), F32),
            pltpu.VMEM((TILE, HALF), F32),
            pltpu.VMEM((CH, COLS), F32),
            pltpu.VMEM((2, TILE, TILE), F32),
            pltpu.VMEM((2 * TILE, 2 * TILE), BF16),
            pltpu.VMEM((2 * TILE, 2 * TILE), BF16),
            pltpu.VMEM((ORDERS, TILE, TILE), F32),
            pltpu.SMEM((6, 3, 1, 6), jnp.int32),
            pltpu.VMEM((3, PART), F32),
            pltpu.VMEM((1, CH), F32),
            pltpu.VMEM((4, TILE), F32),
            dma((6,)),
            dma((9,)),
            dma((PHASES, GROUP)),
            dma((PHASES, GROUP)),
            dma((PHASES, GROUP)),
            dma((PHASES, GROUP)),
            dma((TERMS, PARTS)),
            dma((TERMS, PARTS)),
            dma((TERMS, PARTS)),
            dma((TERMS, PARTS)),
            dma((2, GROUP)),
            dma((2, GROUP)),
        ],
        compiler_params=pltpu.CompilerParams(
            collective_id=0, has_side_effects=True, vmem_limit_bytes=60 * 2**20
        ),
    )(
        counts,
        block_pattern.transpose(1, 2, 0, 3),
        start,
        weights,
        radial_terms,
        energy,
        potential.reshape(4, TILE),
        element_matrices,
    )
    return out.reshape(1, CH, 1, COLS)


def solution(mesh):
    return jax.shard_map(
        shards,
        mesh=mesh,
        in_specs=(
            P("sym", None, "rad", None),
            P("sym", None, None, None, None),
            P("sym", None, None, None),
            P("sym"),
            P(None, "rad"),
            P("sym", None),
            P(),
            P(),
        ),
        out_specs=P("sym", None, "rad", None),
        check_vma=False,
    )
```
